256 devices in a mesh: blk: 32 (over x_hi, z, core), feat: 8 (over x_lo, y).
Axes of the slice: x: 4 (x_hi: 2, x_lo: 2; x = x_hi * 2 + x_lo), y: 4, z: 8, core: 2. Of those that a mesh axis runs over, the one named last changes fastest.
Arguments:
- pool_embed: bfloat16 [262144, 1536], P('blk', 'feat'), may hold values from -16 to 16
- label_embed: bfloat16 [2048, 1536], P('blk', 'feat'), may hold values from -4 to 4
- label_class: int32 [2048], P('blk'), may hold values from 0 to 999
Outputs:
- log_probs: float32 [262144, 1000], P(('blk', 'feat'))
- entropy: float32 [262144], P(('blk', 'feat'))
The draws below stay inside these ranges and needn't reach their ends.
All inputs are finite; a program needn't handle non-finite values.
Results may differ from the reference program's by a relative error of at most 0.0009.
Values may be sent and summed in bfloat16 or wider, within the bound.
No kernel may reach another device: no remote copies, remote signals or barrier semaphores. Data moves between devices by JAX's collectives and lax.ppermute only.
A program may use at most 64 MiB of HBM per device.

```python
import math
import jax
import jax.numpy as jnp
from jax import lax

E = 1536
C = 1000
POOL = 262144
LABELED = 2048


def base_draws(key):
    query_key, label_key = jax.random.split(jax.random.fold_in(key, 17), 2)
    pool_base = jnp.clip(jax.random.normal(query_key, (POOL, E), jnp.float32), -4.0, 4.0)
    label_base = jnp.clip(jax.random.normal(label_key, (LABELED, E), jnp.float32), -4.0, 4.0)
    return (pool_base, label_base)


def draw_pool_embed(key, part):
    pool_base, label_base = base_draws(key)
    return pool_base.astype(jnp.bfloat16)


def draw_label_embed(key, part):
    pool_base, label_base = base_draws(key)
    return label_base.astype(jnp.bfloat16)


def plant(drawn, stream_key, least, top_value):
    extent = drawn.shape
    index_at = [jax.random.randint(jax.random.fold_in(stream_key, axis), (), 0, extent[axis]) for axis in range(len(extent))]
    drawn = drawn.at[tuple(index_at)].set(least)
    longest = extent.index(max(extent))
    index_at[longest] = (index_at[longest] + 1) % extent[longest]
    return drawn.at[tuple(index_at)].set(top_value)


def setup_inputs(seed: int = 0) -> dict:
    key_of = jax.random.split(jax.random.key(seed), 4)
    pool_embed = draw_pool_embed(jax.random.fold_in(key_of[3], 71), 0)
    label_embed = draw_label_embed(jax.random.fold_in(key_of[3], 71), 0)
    label_class = plant(jax.random.randint(key_of[2], (LABELED,), 0, C), jax.random.fold_in(key_of[2], 1), 0, C - 1).astype(jnp.int32)
    return dict(pool_embed=pool_embed, label_embed=label_embed, label_class=label_class)


SMOOTHING = 0.1

def reference(pool_embed, label_embed, label_class):
    scale = 2.0 / math.sqrt(E)
    onehot = (label_class[:, None] == jnp.arange(C, dtype=jnp.int32)[None, :]).astype(jnp.bfloat16)
    block = math.gcd(POOL, 1024)
    grouped = pool_embed.reshape(POOL // block, block, E)

    def one_block(rows_block):
        scores = lax.dot_general(rows_block, label_embed, (((1,), (1,)), ((), ())), preferred_element_type=jnp.float32) * scale
        row_max = lax.optimization_barrier(jnp.max(scores, axis=1))
        weights = jnp.exp(scores - row_max[:, None])
        weight_sum = lax.optimization_barrier(jnp.sum(weights, axis=1))
        class_mass = jnp.dot(weights.astype(jnp.bfloat16), onehot, preferred_element_type=jnp.float32)
        probability = (1.0 - SMOOTHING) * class_mass / weight_sum[:, None] + SMOOTHING / C
        log_probs = jnp.log(probability)
        entropy = -lax.optimization_barrier(jnp.sum(probability * log_probs, axis=1))
        return (log_probs, entropy)
    log_probs, entropy = lax.map(one_block, grouped)
    return (log_probs.reshape(POOL, C), entropy.reshape(POOL))
```

```python
import functools
import math

import jax
import jax.numpy as jnp
from jax import lax
from jax.experimental import pallas as pl
from jax.experimental.pallas import tpu as pltpu
from jax.sharding import Mesh, PartitionSpec as P

C = 1000
SMOOTHING = 0.1
AXES = ("xh", "z", "c", "xl", "y")
SIZES = (2, 8, 2, 2, 4)
PLANE = ("xh", "xl", "y")
FEAT = ("xl", "y")
LANES = 128
TAIL = 16


def shift(x, step):
    n = SIZES[1]
    return lax.ppermute(x, "z", [(i, (i + step) % n) for i in range(n)])


def swap(x):
    return lax.ppermute(x, "c", [(0, 1), (1, 0)])


def arrange_kernel(parts_ref, out_ref):
    half = parts_ref.shape[1]
    rows = 2 * half
    for xh in range(2):
        for j in range(4):
            even = parts_ref[xh * 8 + 2 * j]
            odd = parts_ref[xh * 8 + 2 * j + 1]
            blocks = (
                even[:, :128],
                jnp.concatenate([even[:, 128:192], odd[:, :64]], axis=1),
                odd[:, 64:192],
            )
            for k, block in enumerate(blocks):
                at = (3 * j + k) * rows + xh * half
                out_ref[at : at + half, :] = block
    out_ref[12 * rows :, :] = jnp.concatenate(
        [parts_ref[0, :TAIL, 192:], parts_ref[8, :TAIL, 192:]], axis=1
    )


def arrange(parts):
    rows = 12 * 2 * parts.shape[1] + TAIL
    return pl.pallas_call(
        arrange_kernel,
        out_shape=jax.ShapeDtypeStruct((rows, LANES), parts.dtype),
        cost_estimate=pl.CostEstimate(
            flops=0, bytes_accessed=4 * rows * LANES, transcendentals=0
        ),
    )(parts)


def attend_kernel(pieces, first, last, scale, *refs):
    labels = refs[:pieces]
    pool_ref = refs[pieces]
    refs = refs[pieces + 1 :]
    if not first:
        old_mass, old_stat = refs[:2]
        refs = refs[2:]
    out_ref, stat_ref, keys, onehot = refs
    rows = 128

    @pl.when(pl.program_id(0) == 0)
    def _():
        classes = lax.broadcasted_iota(jnp.int32, (C, rows), 0).astype(jnp.float32)
        for p, ref in enumerate(labels):
            for k in range(12):
                keys[p * rows : (p + 1) * rows, k * 128 : (k + 1) * 128] = ref[
                    k * rows : (k + 1) * rows, :
                ]
            tail = ref[12 * rows :, :].astype(jnp.float32)
            own = tail[0:1] * 32.0 + tail[1:2]
            onehot[:, p * rows : (p + 1) * rows] = jnp.where(
                classes == own, 1.0, 0.0
            ).astype(jnp.bfloat16)

    scores = (
        jnp.dot(keys[...], pool_ref[...], preferred_element_type=jnp.float32) * scale
    )
    top = jnp.max(scores, axis=0, keepdims=True)
    if not first:
        top = jnp.maximum(top, old_stat[0:1])
    weights = jnp.exp(scores - top)
    total = jnp.sum(weights, axis=0, keepdims=True)
    mass = jnp.dot(
        onehot[...], weights.astype(jnp.bfloat16), preferred_element_type=jnp.float32
    )
    if not first:
        fade = jnp.exp(old_stat[0:1] - top)
        total = total + fade * old_stat[1:2]
        mass = mass + fade * old_mass[...]
    if last:
        probability = mass * ((1.0 - SMOOTHING) / total) + SMOOTHING / C
        log_probs = jnp.log(probability)
        out_ref[...] = log_probs
        stat_ref[0:1] = -jnp.sum(probability * log_probs, axis=0, keepdims=True)
    else:
        out_ref[...] = mass
        stat_ref[0:1] = top
        stat_ref[1:2] = total


def attend(pool, labels, state, last, tile=256):
    depth, count = pool.shape
    pieces = len(labels)
    first = state is None
    m = pieces * 128
    mass_spec = pl.BlockSpec((C, tile), lambda i: (0, i))
    stat_spec = pl.BlockSpec((8, tile), lambda i: (0, i))
    in_specs = [pl.BlockSpec(labels[0].shape, lambda i: (0, 0))] * pieces
    in_specs.append(pl.BlockSpec((depth, tile), lambda i: (0, i)))
    args = list(labels) + [pool]
    if not first:
        in_specs += [mass_spec, stat_spec]
        args += list(state)
    return pl.pallas_call(
        functools.partial(
            attend_kernel, pieces, first, last, 2.0 / math.sqrt(depth)
        ),
        grid=(count // tile,),
        in_specs=in_specs,
        out_specs=[mass_spec, stat_spec],
        out_shape=[
            jax.ShapeDtypeStruct((C, count), jnp.float32),
            jax.ShapeDtypeStruct((8, count), jnp.float32),
        ],
        scratch_shapes=[
            pltpu.VMEM((m, depth), jnp.bfloat16),
            pltpu.VMEM((C, m), jnp.bfloat16),
        ],
        compiler_params=pltpu.CompilerParams(vmem_limit_bytes=40 * 2**20),
        cost_estimate=pl.CostEstimate(
            flops=2 * m * count * (depth + C),
            bytes_accessed=m * depth * 2 + depth * count * 2 + 4 * C * count,
            transcendentals=m * count,
        ),
    )(*args)


def per_device(pool_embed, label_embed, label_class):
    feats = 8
    width = pool_embed.shape[1]
    count = pool_embed.shape[0] // feats
    rows = label_embed.shape[0]
    codes = jnp.stack([label_class // 32, label_class % 32]).astype(jnp.bfloat16)
    side = jnp.concatenate([codes, jnp.zeros((rows - 2, rows), jnp.bfloat16)], axis=0)
    own = jnp.concatenate([label_embed, side], axis=1)
    parts = lax.all_to_all(
        jnp.broadcast_to(own[None], (16,) + own.shape), PLANE, 0, 0, tiled=True
    )
    queries = pool_embed.T.reshape(width, feats, count).transpose(1, 0, 2)
    pool = lax.all_to_all(queries, FEAT, 0, 0, tiled=True).reshape(
        feats * width, count
    )
    near = arrange(parts)
    got = [near, swap(near)]
    up, down = near, near
    for _ in range(2):
        up, down = shift(up, 1), shift(down, -1)
        got += [up, down, swap(up), swap(down)]
    state = attend(pool, got, None, False)
    up, down = shift(up, 1), shift(down, -1)
    state = attend(pool, [up, down, swap(up), swap(down)], state, False)
    n = SIZES[1]
    far = jnp.where(lax.axis_index("c") == 0, down, up)
    same = [(2 * i, 2 * ((i - 1) % n)) for i in range(n)]
    same += [(2 * i + 1, 2 * ((i + 1) % n) + 1) for i in range(n)]
    cross = [(a, b ^ 1) for a, b in same]
    ends = [lax.ppermute(far, ("z", "c"), pairs) for pairs in (same, cross)]
    log_probs, stat = attend(pool, ends, state, True)
    return (log_probs.T, stat[0])


def solution(mesh):
    fine = Mesh(mesh.devices.reshape(SIZES), AXES)
    blk, feat = ("xh", "z", "c"), FEAT
    return jax.shard_map(
        per_device,
        mesh=fine,
        in_specs=(P(blk, feat), P(blk, feat), P(blk)),
        out_specs=(P(blk + feat, None), P(blk + feat)),
        check_vma=False,
    )
```

```python
import functools
import math

import jax
import jax.numpy as jnp
from jax import lax
from jax.experimental import pallas as pl
from jax.experimental.pallas import tpu as pltpu
from jax.sharding import Mesh, PartitionSpec as P

C = 1000
SMOOTHING = 0.1
AXES = ("xh", "z", "c", "xl", "y")
SIZES = (2, 8, 2, 2, 4)
FEAT = ("xl", "y")
LANES = 128
TAIL = 16
VMEM = pl.BlockSpec(memory_space=pltpu.VMEM)
ANY = pl.BlockSpec(memory_space=pl.ANY)


def ring(x, axis, step):
    return lax.ppermute(x, axis, [(i, (i + step) % 4) for i in range(4)])


def along_z(x, step, cross=False):
    n = SIZES[1]
    pairs = []
    for i in range(n):
        pairs.append((2 * i, 2 * ((i + step) % n) + cross))
        pairs.append((2 * i + 1, 2 * ((i - step) % n) + 1 - cross))
    return lax.ppermute(x, ("z", "c"), pairs)


def swap(x):
    return lax.ppermute(x, "c", [(0, 1), (1, 0)])


def move(kernel, shape, args, scratch=()):
    return pl.pallas_call(
        kernel,
        out_shape=jax.ShapeDtypeStruct(shape, jnp.bfloat16),
        in_specs=[VMEM] * len(args),
        out_specs=VMEM,
        scratch_shapes=list(scratch),
        cost_estimate=pl.CostEstimate(
            flops=0, bytes_accessed=4 * math.prod(shape), transcendentals=0
        ),
        compiler_params=pltpu.CompilerParams(vmem_limit_bytes=4 * 2**20),
    )(*args)


def pack_kernel(label_ref, class_ref, out_ref):
    rows, width = label_ref.shape
    out_ref[:, :width] = label_ref[...]
    ids = class_ref[...]
    row = lax.broadcasted_iota(jnp.int32, (rows, rows), 0)
    code = jnp.where(row == 0, ids >> 5, jnp.where(row == 1, ids & 31, 0))
    out_ref[:, width:] = code.astype(jnp.float32).astype(jnp.bfloat16)


def along_y_kernel(own_ref, below_ref, above_ref, far_ref, out_ref, parts):
    y = lax.axis_index("y")
    rows = own_ref.shape[0]
    for step, ref in ((0, own_ref), (3, below_ref), (1, above_ref), (2, far_ref)):
        parts[lax.rem(y + step, 4)] = ref[...]
    for j in range(2):
        even, odd = parts[2 * j], parts[2 * j + 1]
        blocks = (
            even[:, :128],
            jnp.concatenate([even[:, 128:192], odd[:, :64]], axis=1),
            odd[:, 64:192],
        )
        for k, block in enumerate(blocks):
            out_ref[(3 * j + k) * rows : (3 * j + k + 1) * rows, :] = block
    tail = own_ref[:TAIL, 192:]
    out_ref[6 * rows :, :] = jnp.concatenate([tail, tail], axis=1)


def along_x_kernel(own_ref, below_ref, above_ref, far_ref, out_ref):
    x = lax.axis_index("xh") * 2 + lax.axis_index("xl")
    half = 64
    for step, ref in ((0, own_ref), (3, below_ref), (1, above_ref), (2, far_ref)):
        at = lax.rem(x + step, 4)
        high, low = at >> 1, at & 1
        for k in range(6):
            row = pl.multiple_of((low * 6 + k) * 2 * half + high * half, half)
            out_ref[pl.ds(row, half), :] = ref[k * half : (k + 1) * half, :]
    own = own_ref[6 * half :, :].astype(jnp.float32)
    far = far_ref[6 * half :, :].astype(jnp.float32)
    lane_high = (lax.broadcasted_iota(jnp.int32, own.shape, 1) >= half).astype(
        jnp.int32
    )
    tail = jnp.where(lane_high == (x >> 1), own, far)
    out_ref[12 * 2 * half :, :] = tail.astype(jnp.bfloat16)


def attend_kernel(pieces, first, last, scale, *refs):
    given = 1 if first else pieces
    labels = refs[:given]
    pool_ref = refs[given]
    refs = refs[given + 1 :]
    if first:
        out_ref, stat_ref, scores, weights, onehot, held, sems = refs
        fetches = [
            pltpu.make_async_copy(labels[0].at[p], held.at[p], sems.at[p])
            for p in range(pieces)
        ]
        for fetch in fetches:
            fetch.start()
        labels = [held.at[p] for p in range(pieces)]
    elif last:
        old_mass, old_stat, out_ref, stat_ref, scores, weights, onehot, logs, sems = refs
    else:
        old_mass, old_stat, out_ref, stat_ref, scores, weights, onehot = refs
    rows = 128
    classes = lax.broadcasted_iota(jnp.int32, (C, rows), 0).astype(jnp.float32)
    top = None if first else old_stat[0:1]
    for pair in range(pieces // 2):
        two = labels[2 * pair : 2 * pair + 2]
        if first:
            fetches[2 * pair].wait()
            fetches[2 * pair + 1].wait()
        keys = jnp.concatenate(
            [
                jnp.concatenate(
                    [ref[k * rows : (k + 1) * rows, :] for ref in two], axis=0
                )
                for k in range(12)
            ],
            axis=1,
        )
        block = (
            jnp.dot(keys, pool_ref[...], preferred_element_type=jnp.float32) * scale
        )
        scores[pair * 2 * rows : (pair + 1) * 2 * rows, :] = block
        high = jnp.max(block, axis=0, keepdims=True)
        top = high if top is None else jnp.maximum(top, high)
        for p, ref in enumerate(two):
            tail = ref[12 * rows :, :].astype(jnp.float32)
            own = tail[0:1] * 32.0 + tail[1:2]
            at = (2 * pair + p) * rows
            onehot[:, at : at + rows] = jnp.where(classes == own, 1.0, 0.0).astype(
                jnp.bfloat16
            )
    total = None
    for pair in range(pieces // 2):
        at = slice(pair * 2 * rows, (pair + 1) * 2 * rows)
        block = jnp.exp(scores[at, :] - top)
        weights[at, :] = block.astype(jnp.bfloat16)
        part = jnp.sum(block, axis=0, keepdims=True)
        total = part if total is None else total + part
    mass = jnp.dot(onehot[...], weights[...], preferred_element_type=jnp.float32)
    if not first:
        fade = jnp.exp(old_stat[0:1] - top)
        total = total + fade * old_stat[1:2]
        mass = mass + fade * old_mass[...]
    if last:
        gain = (1.0 - SMOOTHING) / total
        entropy = jnp.zeros_like(total)
        step = 200
        copies = []
        for i in range(C // step):
            at = slice(i * step, (i + 1) * step)
            probability = mass[at] * gain + SMOOTHING / C
            log_probs = jnp.log(probability)
            logs[at, :] = log_probs
            copies.append(
                pltpu.make_async_copy(logs.at[at], out_ref.at[at], sems.at[i])
            )
            copies[-1].start()
            entropy = entropy - jnp.sum(probability * log_probs, axis=0, keepdims=True)
        stat_ref[...] = entropy
        for copy in copies:
            copy.wait()
    else:
        out_ref[...] = mass
        stat_ref[0:1] = top
        stat_ref[1:2] = total


def attend(pool, labels, state, last):
    depth, count = pool.shape
    first = state is None
    pieces = labels.shape[0] if first else len(labels)
    m = pieces * 128
    args = ([labels] if first else list(labels)) + [pool]
    args += [] if first else list(state)
    scratch = [
        pltpu.VMEM((m, count), jnp.float32),
        pltpu.VMEM((m, count), jnp.bfloat16),
        pltpu.VMEM((C, m), jnp.bfloat16),
    ]
    need = 6 * m * count + 2 * C * m + 4 * C * count
    if first:
        scratch += [
            pltpu.VMEM(labels.shape, jnp.bfloat16),
            pltpu.SemaphoreType.DMA((pieces,)),
        ]
        need += 2 * m * (depth + TAIL)
    if last:
        scratch += [
            pltpu.VMEM((C, count), jnp.float32),
            pltpu.SemaphoreType.DMA((C // 200,)),
        ]
        need += 4 * C * count
    label_specs = [ANY] if first else [VMEM] * pieces
    return pl.pallas_call(
        functools.partial(attend_kernel, pieces, first, last, 2.0 / math.sqrt(depth)),
        in_specs=label_specs + [VMEM] * (len(args) - len(label_specs)),
        out_specs=[ANY if last else VMEM, VMEM],
        out_shape=[
            jax.ShapeDtypeStruct((C, count), jnp.float32),
            jax.ShapeDtypeStruct((1 if last else 2, count), jnp.float32),
        ],
        scratch_shapes=scratch,
        input_output_aliases={}
        if first or last
        else {pieces + 1: 0, pieces + 2: 1},
        compiler_params=pltpu.CompilerParams(vmem_limit_bytes=need + 8 * 2**20),
        cost_estimate=pl.CostEstimate(
            flops=2 * m * count * (depth + C),
            bytes_accessed=4 * C * count,
            transcendentals=m * count,
        ),
    )(*args)


def stash_kernel(count, at, *refs):
    out_ref, sems = refs[-2:]
    copies = [
        pltpu.make_async_copy(refs[i], out_ref.at[at + i], sems.at[i])
        for i in range(count)
    ]
    for copy in copies:
        copy.start()
    for copy in copies:
        copy.wait()


def stash(store, pieces, at, slots):
    shape = (slots,) + pieces[0].shape
    args = list(pieces) + ([] if store is None else [store])
    return pl.pallas_call(
        functools.partial(stash_kernel, len(pieces), at),
        in_specs=[ANY] * len(args),
        out_specs=ANY,
        out_shape=jax.ShapeDtypeStruct(shape, jnp.bfloat16),
        scratch_shapes=[pltpu.SemaphoreType.DMA((len(pieces),))],
        input_output_aliases={} if store is None else {len(pieces): 0},
        cost_estimate=pl.CostEstimate(
            flops=0,
            bytes_accessed=4 * len(pieces) * math.prod(shape[1:]),
            transcendentals=0,
        ),
        compiler_params=pltpu.CompilerParams(vmem_limit_bytes=2**20),
    )(*args)


def split_kernel(in_ref, out_ref, sems):
    parts, _, count = out_ref.shape
    copies = [
        pltpu.make_async_copy(
            in_ref.at[:, p * count : (p + 1) * count], out_ref.at[p], sems.at[p]
        )
        for p in range(parts)
    ]
    for copy in copies:
        copy.start()
    for copy in copies:
        copy.wait()


def split(x, parts):
    width, count = x.shape
    return pl.pallas_call(
        split_kernel,
        in_specs=[ANY],
        out_specs=ANY,
        out_shape=jax.ShapeDtypeStruct((parts, width, count // parts), x.dtype),
        scratch_shapes=[pltpu.SemaphoreType.DMA((parts,))],
        cost_estimate=pl.CostEstimate(
            flops=0, bytes_accessed=4 * width * count, transcendentals=0
        ),
        compiler_params=pltpu.CompilerParams(vmem_limit_bytes=60 * 2**20),
    )(x)


def per_device(pool_embed, label_embed, label_class):
    feats = SIZES[3] * SIZES[4]
    count, width = pool_embed.shape[0] // feats, pool_embed.shape[1]
    rows = label_embed.shape[0]
    own = move(
        pack_kernel, (rows, width + rows), (label_embed, label_class.reshape(1, rows))
    )
    own, pool_embed = lax.optimization_barrier((own, pool_embed))
    pool = lax.all_to_all(split(pool_embed.T, feats), FEAT, 0, 0, tiled=True)
    pool = pool.reshape(feats * width, count)
    near = [own] + [ring(own, "y", step) for step in (1, 3, 2)]
    column = move(
        along_y_kernel,
        (6 * rows + TAIL, LANES),
        near,
        [pltpu.VMEM((4, rows, width + rows), jnp.bfloat16)],
    )
    near = [column] + [ring(column, ("xh", "xl"), step) for step in (1, 3, 2)]
    plane = move(along_x_kernel, (12 * 2 * rows + TAIL, LANES), near)
    other = swap(plane)
    up, down = along_z(plane, 1), along_z(plane, -1)
    store = stash(None, [plane, up, down, other], 0, 10)
    others = [swap(up), swap(down)]
    up, down = along_z(up, 1), along_z(down, -1)
    store = stash(store, others + [up, down], 4, 10)
    store = stash(store, [swap(up), swap(down)], 8, 10)
    state = attend(pool, store, None, False)
    up, down = along_z(up, 1), along_z(down, -1)
    state = attend(pool, [up, down, swap(up), swap(down)], state, False)
    ends = [along_z(up, 1), along_z(up, 1, cross=True)]
    log_probs, entropy = attend(pool, ends, state, True)
    return (log_probs.T, entropy[0])


def solution(mesh):
    fine = Mesh(mesh.devices.reshape(SIZES), AXES)
    blk = ("xh", "z", "c")
    return jax.shard_map(
        per_device,
        mesh=fine,
        in_specs=(P(blk, FEAT), P(blk, FEAT), P(blk)),
        out_specs=(P(blk + FEAT, None), P(blk + FEAT)),
        check_vma=False,
    )
```

```python
import functools
import math

import jax
import jax.numpy as jnp
from jax import lax
from jax.experimental import pallas as pl
from jax.experimental.pallas import tpu as pltpu
from jax.sharding import Mesh, PartitionSpec as P

C = 1000
SMOOTHING = 0.1
AXES = ("xh", "z", "c", "xl", "y")
SIZES = (2, 8, 2, 2, 4)
FEAT = ("xl", "y")
PLANE = ("xh", "xl", "y")
LANES = 128
TAIL = 16
VMEM = pl.BlockSpec(memory_space=pltpu.VMEM)
ANY = pl.BlockSpec(memory_space=pl.ANY)


def along_z(x, step):
    n = SIZES[1]
    return lax.ppermute(x, "z", [(i, (i + step) % n) for i in range(n)])


def outward(x, cross):
    n = SIZES[1]
    pairs = []
    for i in range(n):
        pairs.append((2 * i, 2 * ((i - 1) % n) + cross))
        pairs.append((2 * i + 1, 2 * ((i + 1) % n) + 1 - cross))
    return lax.ppermute(x, ("z", "c"), pairs)


def swap(x):
    return lax.ppermute(x, "c", [(0, 1), (1, 0)])


def move(kernel, shape, args, scratch=()):
    return pl.pallas_call(
        kernel,
        out_shape=jax.ShapeDtypeStruct(shape, jnp.bfloat16),
        in_specs=[VMEM] * len(args),
        out_specs=VMEM,
        scratch_shapes=list(scratch),
        cost_estimate=pl.CostEstimate(
            flops=0, bytes_accessed=4 * math.prod(shape), transcendentals=0
        ),
        compiler_params=pltpu.CompilerParams(vmem_limit_bytes=4 * 2**20),
    )(*args)


def pack_kernel(label_ref, class_ref, out_ref):
    rows, width = label_ref.shape
    ids = class_ref[...]
    row = lax.broadcasted_iota(jnp.int32, (rows, rows), 0)
    code = jnp.where(row == 0, ids >> 5, jnp.where(row == 1, ids & 31, 0))
    block = jnp.concatenate(
        [label_ref[...], code.astype(jnp.float32).astype(jnp.bfloat16)], axis=1
    )
    for i in range(out_ref.shape[0]):
        out_ref[i] = block


def arrange_kernel(parts_ref, out_ref):
    half = parts_ref.shape[1]
    rows = 2 * half
    for xh in range(2):
        for j in range(4):
            even = parts_ref[xh * 8 + 2 * j]
            odd = parts_ref[xh * 8 + 2 * j + 1]
            blocks = (
                even[:, :128],
                jnp.concatenate([even[:, 128:192], odd[:, :64]], axis=1),
                odd[:, 64:192],
            )
            for k, block in enumerate(blocks):
                at = (3 * j + k) * rows + xh * half
                out_ref[at : at + half, :] = block
    out_ref[12 * rows :, :] = jnp.concatenate(
        [parts_ref[0, :TAIL, 192:], parts_ref[8, :TAIL, 192:]], axis=1
    )


def attend_kernel(pieces, first, last, scale, *refs):
    given = 1 if first else pieces
    labels = refs[:given]
    pool_ref = refs[given]
    refs = refs[given + 1 :]
    if first:
        out_ref, stat_ref, scores, weights, onehot = refs
        labels = [labels[0].at[p] for p in range(pieces)]
    elif last:
        old_mass, old_stat, out_ref, stat_ref, scores, weights, onehot, logs, sems = refs
    else:
        old_mass, old_stat, out_ref, stat_ref, scores, weights, onehot = refs
    rows = 128
    classes = lax.broadcasted_iota(jnp.int32, (C, rows), 0).astype(jnp.float32)
    top = None if first else old_stat[0:1]
    for pair in range(pieces // 2):
        two = labels[2 * pair : 2 * pair + 2]
        keys = jnp.concatenate(
            [
                jnp.concatenate(
                    [ref[k * rows : (k + 1) * rows, :] for ref in two], axis=0
                )
                for k in range(12)
            ],
            axis=1,
        )
        block = (
            jnp.dot(keys, pool_ref[...], preferred_element_type=jnp.float32) * scale
        )
        scores[pair * 2 * rows : (pair + 1) * 2 * rows, :] = block
        high = jnp.max(block, axis=0, keepdims=True)
        top = high if top is None else jnp.maximum(top, high)
        for p, ref in enumerate(two):
            tail = ref[12 * rows :, :].astype(jnp.float32)
            own = tail[0:1] * 32.0 + tail[1:2]
            at = (2 * pair + p) * rows
            onehot[:, at : at + rows] = jnp.where(classes == own, 1.0, 0.0).astype(
                jnp.bfloat16
            )
    total = None
    for pair in range(pieces // 2):
        at = slice(pair * 2 * rows, (pair + 1) * 2 * rows)
        block = jnp.exp(scores[at, :] - top)
        weights[at, :] = block.astype(jnp.bfloat16)
        part = jnp.sum(block, axis=0, keepdims=True)
        total = part if total is None else total + part
    mass = jnp.dot(onehot[...], weights[...], preferred_element_type=jnp.float32)
    if not first:
        fade = jnp.exp(old_stat[0:1] - top)
        total = total + fade * old_stat[1:2]
        mass = mass + fade * old_mass[...]
    if last:
        gain = (1.0 - SMOOTHING) / total
        entropy = jnp.zeros_like(total)
        step = 200
        copies = []
        for i in range(C // step):
            at = slice(i * step, (i + 1) * step)
            probability = mass[at] * gain + SMOOTHING / C
            log_probs = jnp.log(probability)
            logs[at, :] = log_probs
            copies.append(
                pltpu.make_async_copy(logs.at[at], out_ref.at[at], sems.at[i])
            )
            copies[-1].start()
            entropy = entropy - jnp.sum(probability * log_probs, axis=0, keepdims=True)
        stat_ref[...] = entropy
        for copy in copies:
            copy.wait()
    else:
        out_ref[...] = mass
        stat_ref[0:1] = top
        stat_ref[1:2] = total


def attend(pool, labels, state, last):
    depth, count = pool.shape
    first = state is None
    pieces = labels.shape[0] if first else len(labels)
    m = pieces * 128
    args = ([labels] if first else list(labels)) + [pool]
    args += [] if first else list(state)
    scratch = [
        pltpu.VMEM((m, count), jnp.float32),
        pltpu.VMEM((m, count), jnp.bfloat16),
        pltpu.VMEM((C, m), jnp.bfloat16),
    ]
    need = 6 * m * count + 2 * C * m + 4 * C * count
    if last:
        scratch += [
            pltpu.VMEM((C, count), jnp.float32),
            pltpu.SemaphoreType.DMA((C // 200,)),
        ]
        need += 4 * C * count
    label_specs = [VMEM] if first else [VMEM] * pieces
    return pl.pallas_call(
        functools.partial(attend_kernel, pieces, first, last, 2.0 / math.sqrt(depth)),
        in_specs=label_specs + [VMEM] * (len(args) - len(label_specs)),
        out_specs=[ANY if last else VMEM, VMEM],
        out_shape=[
            jax.ShapeDtypeStruct((C, count), jnp.float32),
            jax.ShapeDtypeStruct((1 if last else 2, count), jnp.float32),
        ],
        scratch_shapes=scratch,
        input_output_aliases={}
        if first or last
        else {pieces + 1: 0, pieces + 2: 1},
        compiler_params=pltpu.CompilerParams(vmem_limit_bytes=need + 8 * 2**20),
        cost_estimate=pl.CostEstimate(
            flops=2 * m * count * (depth + C),
            bytes_accessed=4 * C * count,
            transcendentals=m * count,
        ),
    )(*args)


def stash_kernel(count, at, *refs):
    out_ref, sems = refs[-2:]
    copies = [
        pltpu.make_async_copy(refs[i], out_ref.at[at + i], sems.at[i])
        for i in range(count)
    ]
    for copy in copies:
        copy.start()
    for copy in copies:
        copy.wait()


def stash(store, pieces, at, slots):
    shape = (slots,) + pieces[0].shape
    args = list(pieces) + ([] if store is None else [store])
    return pl.pallas_call(
        functools.partial(stash_kernel, len(pieces), at),
        in_specs=[ANY] * len(args),
        out_specs=ANY,
        out_shape=jax.ShapeDtypeStruct(shape, jnp.bfloat16),
        scratch_shapes=[pltpu.SemaphoreType.DMA((len(pieces),))],
        input_output_aliases={} if store is None else {len(pieces): 0},
        cost_estimate=pl.CostEstimate(
            flops=0,
            bytes_accessed=4 * len(pieces) * math.prod(shape[1:]),
            transcendentals=0,
        ),
        compiler_params=pltpu.CompilerParams(vmem_limit_bytes=60 * 2**20),
    )(*args)


def choose_kernel(up_ref, down_ref, out_ref, sem):
    core = lax.axis_index("c")

    @pl.when(core == 0)
    def _():
        copy = pltpu.make_async_copy(down_ref, out_ref, sem)
        copy.start()
        copy.wait()

    @pl.when(core != 0)
    def _():
        copy = pltpu.make_async_copy(up_ref, out_ref, sem)
        copy.start()
        copy.wait()


def choose(up, down):
    return pl.pallas_call(
        choose_kernel,
        in_specs=[ANY, ANY],
        out_specs=ANY,
        out_shape=jax.ShapeDtypeStruct(up.shape, up.dtype),
        scratch_shapes=[pltpu.SemaphoreType.DMA],
        cost_estimate=pl.CostEstimate(
            flops=0, bytes_accessed=4 * up.size, transcendentals=0
        ),
        compiler_params=pltpu.CompilerParams(vmem_limit_bytes=2**20),
    )(up, down)


def per_device(pool_embed, label_embed, label_class):
    feats = SIZES[3] * SIZES[4]
    count, width = pool_embed.shape[0] // feats, pool_embed.shape[1]
    rows = label_embed.shape[0]
    own = move(
        pack_kernel,
        (16, rows, width + rows),
        (label_embed, label_class.reshape(1, rows)),
    )
    parts = lax.all_to_all(own, PLANE, 0, 0, tiled=True)
    own, pool_embed = lax.optimization_barrier((own, pool_embed))
    queries = pool_embed.T.reshape(width, feats, count).transpose(1, 0, 2)
    pool = lax.all_to_all(queries, FEAT, 0, 0, tiled=True)
    pool = pool.reshape(feats * width, count)
    plane = move(arrange_kernel, (12 * 2 * rows + TAIL, LANES), (parts,))
    slots = 14
    up, down = along_z(plane, 1), along_z(plane, -1)
    store = stash(None, [plane, swap(plane), up, down], 0, slots)
    others = [swap(up), swap(down)]
    up, down = along_z(up, 1), along_z(down, -1)
    store = stash(store, others + [up, down], 4, slots)
    others = [swap(up), swap(down)]
    up, down = along_z(up, 1), along_z(down, -1)
    store = stash(store, others + [up, down, swap(up), swap(down)], 8, slots)
    far = choose(up, down)
    ends = [outward(far, 0), outward(far, 1)]
    state = attend(pool, store, None, False)
    log_probs, entropy = attend(pool, ends, state, True)
    return (log_probs.T, entropy[0])


def solution(mesh):
    fine = Mesh(mesh.devices.reshape(SIZES), AXES)
    blk = ("xh", "z", "c")
    return jax.shard_map(
        per_device,
        mesh=fine,
        in_specs=(P(blk, FEAT), P(blk, FEAT), P(blk)),
        out_specs=(P(blk + FEAT, None), P(blk + FEAT)),
        check_vma=False,
    )
```

```python
import functools
import math

import jax
import jax.numpy as jnp
from jax import lax
from jax.experimental import pallas as pl
from jax.experimental.pallas import tpu as pltpu
from jax.sharding import Mesh, PartitionSpec as P

C = 1000
SMOOTHING = 0.1
AXES = ("xh", "z", "c", "xl", "y")
SIZES = (2, 8, 2, 2, 4)
FEAT = ("xl", "y")
PLANE = ("xh", "xl", "y")
LANES = 128
TAIL = 16
VMEM = pl.BlockSpec(memory_space=pltpu.VMEM)
ANY = pl.BlockSpec(memory_space=pl.ANY)


def along_z(x, step):
    n = SIZES[1]
    return lax.ppermute(x, "z", [(i, (i + step) % n) for i in range(n)])


def outward(x, cross):
    n = SIZES[1]
    pairs = []
    for i in range(n):
        pairs.append((2 * i, 2 * ((i - 1) % n) + cross))
        pairs.append((2 * i + 1, 2 * ((i + 1) % n) + 1 - cross))
    return lax.ppermute(x, ("z", "c"), pairs)


def swap(x):
    return lax.ppermute(x, "c", [(0, 1), (1, 0)])


def move(kernel, shape, args, vmem=4):
    return pl.pallas_call(
        kernel,
        out_shape=jax.ShapeDtypeStruct(shape, jnp.bfloat16),
        in_specs=[VMEM] * len(args),
        out_specs=VMEM,
        cost_estimate=pl.CostEstimate(
            flops=0, bytes_accessed=4 * math.prod(shape), transcendentals=0
        ),
        compiler_params=pltpu.CompilerParams(vmem_limit_bytes=vmem * 2**20),
    )(*args)


def pack_kernel(label_ref, class_ref, out_ref):
    rows, width = label_ref.shape
    ids = class_ref[...]
    row = lax.broadcasted_iota(jnp.int32, (rows, rows), 0)
    code = jnp.where(row == 0, ids >> 5, jnp.where(row == 1, ids & 31, 0))
    block = jnp.concatenate(
        [label_ref[...], code.astype(jnp.float32).astype(jnp.bfloat16)], axis=1
    )
    for i in range(out_ref.shape[0]):
        out_ref[i] = block


def arrange_kernel(parts_ref, out_ref):
    half = parts_ref.shape[1]
    rows = 2 * half
    for xh in range(2):
        for j in range(4):
            even = parts_ref[xh * 8 + 2 * j]
            odd = parts_ref[xh * 8 + 2 * j + 1]
            blocks = (
                even[:, :128],
                jnp.concatenate([even[:, 128:192], odd[:, :64]], axis=1),
                odd[:, 64:192],
            )
            for k, block in enumerate(blocks):
                at = (3 * j + k) * rows + xh * half
                out_ref[at : at + half, :] = block
    out_ref[12 * rows :, :] = jnp.concatenate(
        [parts_ref[0, :TAIL, 192:], parts_ref[8, :TAIL, 192:]], axis=1
    )


def attend_kernel(pieces, first, last, scale, *refs):
    labels = refs[:pieces]
    pool_ref = refs[pieces]
    refs = refs[pieces + 1 :]
    if first:
        out_ref, stat_ref, scores, weights, onehot, held, sems = refs
        fetches = [
            pltpu.make_async_copy(ref, held.at[p], sems.at[p])
            for p, ref in enumerate(labels)
        ]
        for fetch in fetches:
            fetch.start()
        labels = [held.at[p] for p in range(pieces)]
    elif last:
        old_mass, old_stat, out_ref, stat_ref, scores, weights, onehot, logs, sems = refs
    else:
        old_mass, old_stat, out_ref, stat_ref, scores, weights, onehot = refs
    rows = 128
    classes = lax.broadcasted_iota(jnp.int32, (C, rows), 0).astype(jnp.float32)
    top = None if first else old_stat[0:1]
    for pair in range(pieces // 2):
        two = labels[2 * pair : 2 * pair + 2]
        if first:
            fetches[2 * pair].wait()
            fetches[2 * pair + 1].wait()
        keys = jnp.concatenate(
            [
                jnp.concatenate(
                    [ref[k * rows : (k + 1) * rows, :] for ref in two], axis=0
                )
                for k in range(12)
            ],
            axis=1,
        )
        block = (
            jnp.dot(keys, pool_ref[...], preferred_element_type=jnp.float32) * scale
        )
        scores[pair * 2 * rows : (pair + 1) * 2 * rows, :] = block
        high = jnp.max(block, axis=0, keepdims=True)
        top = high if top is None else jnp.maximum(top, high)
        for p, ref in enumerate(two):
            tail = ref[12 * rows :, :].astype(jnp.float32)
            own = tail[0:1] * 32.0 + tail[1:2]
            at = (2 * pair + p) * rows
            onehot[:, at : at + rows] = jnp.where(classes == own, 1.0, 0.0).astype(
                jnp.bfloat16
            )
    total = None
    for pair in range(pieces // 2):
        at = slice(pair * 2 * rows, (pair + 1) * 2 * rows)
        block = jnp.exp(scores[at, :] - top)
        weights[at, :] = block.astype(jnp.bfloat16)
        part = jnp.sum(block, axis=0, keepdims=True)
        total = part if total is None else total + part
    if not first:
        fade = jnp.exp(old_stat[0:1] - top)
        total = total + fade * old_stat[1:2]
    if last:
        gain = (1.0 - SMOOTHING) / total
        kept = fade * gain
        entropy = jnp.zeros_like(total)
        step = 200
        copies = []
        for i in range(C // step):
            at = slice(i * step, (i + 1) * step)
            mass = jnp.dot(
                onehot[at, :], weights[...], preferred_element_type=jnp.float32
            )
            probability = mass * gain + (old_mass[at, :] * kept + SMOOTHING / C)
            log_probs = jnp.log(probability)
            logs[at, :] = log_probs
            copies.append(
                pltpu.make_async_copy(logs.at[at], out_ref.at[at], sems.at[i])
            )
            copies[-1].start()
            entropy = entropy - jnp.sum(probability * log_probs, axis=0, keepdims=True)
        stat_ref[...] = entropy
        for copy in copies:
            copy.wait()
    else:
        mass = jnp.dot(onehot[...], weights[...], preferred_element_type=jnp.float32)
        out_ref[...] = mass if first else mass + fade * old_mass[...]
        stat_ref[0:1] = top
        stat_ref[1:2] = total


def attend(pool, labels, state, last):
    depth, count = pool.shape
    first = state is None
    pieces = len(labels)
    m = pieces * 128
    pool = pltpu.with_memory_space_constraint(pool, pltpu.VMEM)
    args = list(labels) + [pool] + ([] if first else list(state))
    scratch = [
        pltpu.VMEM((m, count), jnp.float32),
        pltpu.VMEM((m, count), jnp.bfloat16),
        pltpu.VMEM((C, m), jnp.bfloat16),
    ]
    need = 6 * m * count + 2 * C * m + 4 * C * count
    if first:
        scratch += [
            pltpu.VMEM((pieces,) + labels[0].shape, jnp.bfloat16),
            pltpu.SemaphoreType.DMA((pieces,)),
        ]
    if last:
        scratch += [
            pltpu.VMEM((C, count), jnp.float32),
            pltpu.SemaphoreType.DMA((C // 200,)),
        ]
        need += 4 * C * count
    label_specs = [ANY if first else VMEM] * pieces
    place = jax.ShapeDtypeStruct if last else pltpu.VMEM
    return pl.pallas_call(
        functools.partial(attend_kernel, pieces, first, last, 2.0 / math.sqrt(depth)),
        in_specs=label_specs + [VMEM] * (len(args) - len(label_specs)),
        out_specs=[ANY if last else VMEM, VMEM],
        out_shape=[
            place((C, count), jnp.float32),
            place((1 if last else 2, count), jnp.float32),
        ],
        scratch_shapes=scratch,
        input_output_aliases={}
        if first or last
        else {pieces + 1: 0, pieces + 2: 1},
        compiler_params=pltpu.CompilerParams(vmem_limit_bytes=53 * 2**20 if first else need + 8 * 2**20),
        cost_estimate=pl.CostEstimate(
            flops=2 * m * count * (depth + C),
            bytes_accessed=4 * C * count,
            transcendentals=m * count,
        ),
    )(*args)


def choose_kernel(up_ref, down_ref, out_ref):
    core = lax.axis_index("c")

    @pl.when(core == 0)
    def _():
        out_ref[...] = down_ref[...]

    @pl.when(core != 0)
    def _():
        out_ref[...] = up_ref[...]


def per_device(pool_embed, label_embed, label_class):
    feats = SIZES[3] * SIZES[4]
    count, width = pool_embed.shape[0] // feats, pool_embed.shape[1]
    rows = label_embed.shape[0]
    own = move(
        pack_kernel,
        (16, rows, width + rows),
        (label_embed, label_class.reshape(1, rows)),
        60,
    )
    parts = lax.all_to_all(own, PLANE, 0, 0, tiled=True)
    own, pool_embed = lax.optimization_barrier((own, pool_embed))
    queries = pool_embed.T.reshape(width, feats, count).transpose(1, 0, 2)
    plane = move(arrange_kernel, (12 * 2 * rows + TAIL, LANES), (parts,))
    plane, queries = lax.optimization_barrier((plane, queries))
    pool = lax.all_to_all(queries, FEAT, 0, 0, tiled=True)
    pool = pool.reshape(feats * width, count)
    got = [plane, swap(plane)]
    up, down = plane, plane
    for _ in range(3):
        up, down = along_z(up, 1), along_z(down, -1)
        got += [up, down, swap(up), swap(down)]
    far = move(choose_kernel, up.shape, (up, down))
    ends = [outward(far, 0), outward(far, 1)]
    state = attend(pool, got, None, False)
    log_probs, entropy = attend(pool, ends, state, True)
    return (log_probs.T, entropy[0])


def solution(mesh):
    fine = Mesh(mesh.devices.reshape(SIZES), AXES)
    blk = ("xh", "z", "c")
    return jax.shard_map(
        per_device,
        mesh=fine,
        in_specs=(P(blk, FEAT), P(blk, FEAT), P(blk)),
        out_specs=(P(blk + FEAT, None), P(blk + FEAT)),
        check_vma=False,
    )
```

```python
import functools
import math

import jax
import jax.numpy as jnp
from jax import lax
from jax.experimental import pallas as pl
from jax.experimental.pallas import tpu as pltpu
from jax.sharding import Mesh, PartitionSpec as P

C = 1000
SMOOTHING = 0.1
AXES = ("xh", "z", "c", "xl", "y")
SIZES = (2, 8, 2, 2, 4)
FEAT = ("xl", "y")
PLANE = ("xh", "xl", "y")
LANES = 128
TAIL = 16
VMEM = pl.BlockSpec(memory_space=pltpu.VMEM)
ANY = pl.BlockSpec(memory_space=pl.ANY)


def along_z(x, step):
    n = SIZES[1]
    return lax.ppermute(x, "z", [(i, (i + step) % n) for i in range(n)])


def outward(x, cross):
    n = SIZES[1]
    pairs = []
    for i in range(n):
        pairs.append((2 * i, 2 * ((i - 1) % n) + cross))
        pairs.append((2 * i + 1, 2 * ((i + 1) % n) + 1 - cross))
    return lax.ppermute(x, ("z", "c"), pairs)


def swap(x):
    return lax.ppermute(x, "c", [(0, 1), (1, 0)])


def move(kernel, shape, args, vmem=4):
    return pl.pallas_call(
        kernel,
        out_shape=jax.ShapeDtypeStruct(shape, jnp.bfloat16),
        in_specs=[VMEM] * len(args),
        out_specs=VMEM,
        cost_estimate=pl.CostEstimate(
            flops=0, bytes_accessed=4 * math.prod(shape), transcendentals=0
        ),
        compiler_params=pltpu.CompilerParams(vmem_limit_bytes=vmem * 2**20),
    )(*args)


def pack_kernel(label_ref, class_ref, out_ref):
    rows, width = label_ref.shape
    ids = class_ref[...]
    row = lax.broadcasted_iota(jnp.int32, (rows, rows), 0)
    code = jnp.where(row == 0, ids >> 5, jnp.where(row == 1, ids & 31, 0))
    block = jnp.concatenate(
        [label_ref[...], code.astype(jnp.float32).astype(jnp.bfloat16)], axis=1
    )
    for i in range(out_ref.shape[0]):
        out_ref[i] = block


def arrange_kernel(parts_ref, out_ref):
    half = parts_ref.shape[1]
    rows = 2 * half
    for xh in range(2):
        for j in range(4):
            even = parts_ref[xh * 8 + 2 * j]
            odd = parts_ref[xh * 8 + 2 * j + 1]
            blocks = (
                even[:, :128],
                jnp.concatenate([even[:, 128:192], odd[:, :64]], axis=1),
                odd[:, 64:192],
            )
            for k, block in enumerate(blocks):
                at = (3 * j + k) * rows + xh * half
                out_ref[at : at + half, :] = block
    out_ref[12 * rows :, :] = jnp.concatenate(
        [parts_ref[0, :TAIL, 192:], parts_ref[8, :TAIL, 192:]], axis=1
    )


def attend_kernel(pieces, first, last, scale, *refs):
    labels = refs[:pieces]
    pool_ref = refs[pieces]
    refs = refs[pieces + 1 :]
    if first:
        out_ref, stat_ref, scores, weights, onehot, held, sems = refs
        fetches = [
            pltpu.make_async_copy(ref, held.at[p], sems.at[p])
            for p, ref in enumerate(labels)
        ]
        for fetch in fetches:
            fetch.start()
        labels = [held.at[p] for p in range(pieces)]
    elif last:
        old_mass, old_stat, out_ref, stat_ref, scores, weights, onehot, logs, sems = refs
    else:
        old_mass, old_stat, out_ref, stat_ref, scores, weights, onehot = refs
    rows = 128
    classes = lax.broadcasted_iota(jnp.int32, (C, rows), 0).astype(jnp.float32)
    top = None if first else old_stat[0:1]
    for pair in range(pieces // 2):
        two = labels[2 * pair : 2 * pair + 2]
        if first:
            for fetch in {0: fetches[:4], 2: fetches[4:]}.get(pair, []):
                fetch.wait()
        keys = jnp.concatenate(
            [
                jnp.concatenate(
                    [ref[k * rows : (k + 1) * rows, :] for ref in two], axis=0
                )
                for k in range(12)
            ],
            axis=1,
        )
        block = (
            jnp.dot(keys, pool_ref[...], preferred_element_type=jnp.float32) * scale
        )
        scores[pair * 2 * rows : (pair + 1) * 2 * rows, :] = block
        high = jnp.max(block, axis=0, keepdims=True)
        top = high if top is None else jnp.maximum(top, high)
        for p, ref in enumerate(two):
            tail = ref[12 * rows :, :].astype(jnp.float32)
            own = tail[0:1] * 32.0 + tail[1:2]
            at = (2 * pair + p) * rows
            onehot[:, at : at + rows] = jnp.where(classes == own, 1.0, 0.0).astype(
                jnp.bfloat16
            )
    total = None
    for pair in range(pieces // 2):
        at = slice(pair * 2 * rows, (pair + 1) * 2 * rows)
        block = jnp.exp(scores[at, :] - top)
        weights[at, :] = block.astype(jnp.bfloat16)
        part = jnp.sum(block, axis=0, keepdims=True)
        total = part if total is None else total + part
    if not first:
        fade = jnp.exp(old_stat[0:1] - top)
        total = total + fade * old_stat[1:2]
    if last:
        gain = (1.0 - SMOOTHING) / total
        kept = fade * gain
        entropy = jnp.zeros_like(total)
        step = 200
        copies = []
        for i in range(C // step):
            at = slice(i * step, (i + 1) * step)
            mass = jnp.dot(
                onehot[at, :], weights[...], preferred_element_type=jnp.float32
            )
            probability = mass * gain + (old_mass[at, :] * kept + SMOOTHING / C)
            log_probs = jnp.log(probability)
            logs[at, :] = log_probs
            copies.append(
                pltpu.make_async_copy(logs.at[at], out_ref.at[at], sems.at[i])
            )
            copies[-1].start()
            entropy = entropy - jnp.sum(probability * log_probs, axis=0, keepdims=True)
        stat_ref[...] = entropy
        for copy in copies:
            copy.wait()
    else:
        mass = jnp.dot(onehot[...], weights[...], preferred_element_type=jnp.float32)
        out_ref[...] = mass if first else mass + fade * old_mass[...]
        stat_ref[0:1] = top
        stat_ref[1:2] = total


def attend(pool, labels, state, last):
    depth, count = pool.shape
    first = state is None
    pieces = len(labels)
    m = pieces * 128
    pool = pltpu.with_memory_space_constraint(pool, pltpu.VMEM)
    args = list(labels) + [pool] + ([] if first else list(state))
    scratch = [
        pltpu.VMEM((m, count), jnp.float32),
        pltpu.VMEM((m, count), jnp.bfloat16),
        pltpu.VMEM((C, m), jnp.bfloat16),
    ]
    need = 6 * m * count + 2 * C * m + 4 * C * count
    if first:
        scratch += [
            pltpu.VMEM((pieces,) + labels[0].shape, jnp.bfloat16),
            pltpu.SemaphoreType.DMA((pieces,)),
        ]
    if last:
        scratch += [
            pltpu.VMEM((C, count), jnp.float32),
            pltpu.SemaphoreType.DMA((C // 200,)),
        ]
        need += 4 * C * count
    label_specs = [ANY if first else VMEM] * pieces
    place = jax.ShapeDtypeStruct if last else pltpu.VMEM
    return pl.pallas_call(
        functools.partial(attend_kernel, pieces, first, last, 2.0 / math.sqrt(depth)),
        in_specs=label_specs + [VMEM] * (len(args) - len(label_specs)),
        out_specs=[ANY if last else VMEM, VMEM],
        out_shape=[
            place((C, count), jnp.float32),
            place((1 if last else 2, count), jnp.float32),
        ],
        scratch_shapes=scratch,
        input_output_aliases={}
        if first or last
        else {pieces + 1: 0, pieces + 2: 1},
        compiler_params=pltpu.CompilerParams(vmem_limit_bytes=52 * 2**20 if first else need + 8 * 2**20),
        cost_estimate=pl.CostEstimate(
            flops=2 * m * count * (depth + C),
            bytes_accessed=4 * C * count,
            transcendentals=m * count,
        ),
    )(*args)


def choose_kernel(up_ref, down_ref, out_ref):
    core = lax.axis_index("c")

    @pl.when(core == 0)
    def _():
        out_ref[...] = down_ref[...]

    @pl.when(core != 0)
    def _():
        out_ref[...] = up_ref[...]


def per_device(pool_embed, label_embed, label_class):
    feats = SIZES[3] * SIZES[4]
    count, width = pool_embed.shape[0] // feats, pool_embed.shape[1]
    rows = label_embed.shape[0]
    own = move(
        pack_kernel,
        (16, rows, width + rows),
        (label_embed, label_class.reshape(1, rows)),
        60,
    )
    parts = lax.all_to_all(own, PLANE, 0, 0, tiled=True)
    own, pool_embed = lax.optimization_barrier((own, pool_embed))
    queries = pool_embed.T.reshape(width, feats, count).transpose(1, 0, 2)
    plane = move(arrange_kernel, (12 * 2 * rows + TAIL, LANES), (parts,))
    plane, queries = lax.optimization_barrier((plane, queries))
    pool = lax.all_to_all(queries, FEAT, 0, 0, tiled=True)
    pool = pool.reshape(feats * width, count)
    got = [plane, swap(plane)]
    up, down = plane, plane
    for _ in range(3):
        up, down = along_z(up, 1), along_z(down, -1)
        got += [up, down, swap(up), swap(down)]
    far = move(choose_kernel, up.shape, (up, down))
    ends = [
        pltpu.with_memory_space_constraint(outward(far, cross), pltpu.VMEM)
        for cross in (0, 1)
    ]
    state = attend(pool, got, None, False)
    log_probs, entropy = attend(pool, ends, state, True)
    return (log_probs.T, entropy[0])


def solution(mesh):
    fine = Mesh(mesh.devices.reshape(SIZES), AXES)
    blk = ("xh", "z", "c")
    return jax.shard_map(
        per_device,
        mesh=fine,
        in_specs=(P(blk, FEAT), P(blk, FEAT), P(blk)),
        out_specs=(P(blk + FEAT, None), P(blk + FEAT)),
        check_vma=False,
    )
```

```python
import functools
import math

import jax
import jax.numpy as jnp
from jax import lax
from jax.experimental import pallas as pl
from jax.experimental.pallas import tpu as pltpu
from jax.sharding import Mesh, PartitionSpec as P

C = 1000
SMOOTHING = 0.1
AXES = ("xh", "z", "c", "xl", "y")
SIZES = (2, 8, 2, 2, 4)
FEAT = ("xl", "y")
PLANE = ("xh", "xl", "y")
LANES = 128
TAIL = 16
VMEM = pl.BlockSpec(memory_space=pltpu.VMEM)
ANY = pl.BlockSpec(memory_space=pl.ANY)


def along_z(x, step):
    n = SIZES[1]
    return lax.ppermute(x, "z", [(i, (i + step) % n) for i in range(n)])


def outward(x, cross):
    n = SIZES[1]
    pairs = []
    for i in range(n):
        pairs.append((2 * i, 2 * ((i - 1) % n) + cross))
        pairs.append((2 * i + 1, 2 * ((i + 1) % n) + 1 - cross))
    return lax.ppermute(x, ("z", "c"), pairs)


def swap(x):
    return lax.ppermute(x, "c", [(0, 1), (1, 0)])


def move(kernel, shape, args, vmem=4):
    return pl.pallas_call(
        kernel,
        out_shape=jax.ShapeDtypeStruct(shape, jnp.bfloat16),
        in_specs=[VMEM] * len(args),
        out_specs=VMEM,
        cost_estimate=pl.CostEstimate(
            flops=0, bytes_accessed=4 * math.prod(shape), transcendentals=0
        ),
        compiler_params=pltpu.CompilerParams(vmem_limit_bytes=vmem * 2**20),
    )(*args)


def pack_kernel(label_ref, class_ref, out_ref):
    rows, width = label_ref.shape
    ids = class_ref[...]
    row = lax.broadcasted_iota(jnp.int32, (rows, rows), 0)
    code = jnp.where(row == 0, ids >> 5, jnp.where(row == 1, ids & 31, 0))
    block = jnp.concatenate(
        [label_ref[...], code.astype(jnp.float32).astype(jnp.bfloat16)], axis=1
    )
    for i in range(out_ref.shape[0]):
        out_ref[i] = block


def arrange_kernel(parts_ref, out_ref):
    half = parts_ref.shape[1]
    rows = 2 * half
    for xh in range(2):
        for j in range(4):
            even = parts_ref[xh * 8 + 2 * j]
            odd = parts_ref[xh * 8 + 2 * j + 1]
            blocks = (
                even[:, :128],
                jnp.concatenate([even[:, 128:192], odd[:, :64]], axis=1),
                odd[:, 64:192],
            )
            for k, block in enumerate(blocks):
                at = (3 * j + k) * rows + xh * half
                out_ref[at : at + half, :] = block
    out_ref[12 * rows :, :] = jnp.concatenate(
        [parts_ref[0, :TAIL, 192:], parts_ref[8, :TAIL, 192:]], axis=1
    )


def attend_kernel(pieces, first, last, scale, *refs):
    labels = refs[:pieces]
    pool_ref = refs[pieces]
    refs = refs[pieces + 1 :]
    if first:
        out_ref, stat_ref, scores, weights, onehot, held, sems = refs
        fetches = [
            pltpu.make_async_copy(ref, held.at[p], sems.at[p])
            for p, ref in enumerate(labels)
        ]
        for fetch in fetches:
            fetch.start()
        labels = [held.at[p] for p in range(pieces)]
    elif last:
        old_mass, old_stat, out_ref, stat_ref, scores, weights, onehot, logs, sems = refs
    else:
        old_mass, old_stat, out_ref, stat_ref, scores, weights, onehot = refs
    rows = 128
    classes = lax.broadcasted_iota(jnp.int32, (C, rows), 0).astype(jnp.float32)
    top = None if first else old_stat[0:1]
    for pair in range(pieces // 2):
        two = labels[2 * pair : 2 * pair + 2]
        if first:
            for fetch in {0: fetches[:4], 2: fetches[4:]}.get(pair, []):
                fetch.wait()
        keys = jnp.concatenate(
            [
                jnp.concatenate(
                    [ref[k * rows : (k + 1) * rows, :] for ref in two], axis=0
                )
                for k in range(12)
            ],
            axis=1,
        )
        block = (
            jnp.dot(keys, pool_ref[...], preferred_element_type=jnp.float32) * scale
        )
        scores[pair * 2 * rows : (pair + 1) * 2 * rows, :] = block
        high = jnp.max(block, axis=0, keepdims=True)
        top = high if top is None else jnp.maximum(top, high)
        for p, ref in enumerate(two):
            tail = ref[12 * rows :, :].astype(jnp.float32)
            own = tail[0:1] * 32.0 + tail[1:2]
            at = (2 * pair + p) * rows
            onehot[:, at : at + rows] = jnp.where(classes == own, 1.0, 0.0).astype(
                jnp.bfloat16
            )
    total = None
    for pair in range(pieces // 2):
        at = slice(pair * 2 * rows, (pair + 1) * 2 * rows)
        block = jnp.exp2(scores[at, :] - top)
        weights[at, :] = block.astype(jnp.bfloat16)
        part = jnp.sum(block, axis=0, keepdims=True)
        total = part if total is None else total + part
    if not first:
        fade = jnp.exp2(old_stat[0:1] - top)
        total = total + fade * old_stat[1:2]
    if last:
        gain = (1.0 - SMOOTHING) / total
        kept = fade * gain
        entropy = jnp.zeros_like(total)
        step = 200
        copies = []
        for i in range(C // step):
            at = slice(i * step, (i + 1) * step)
            mass = jnp.dot(
                onehot[at, :], weights[...], preferred_element_type=jnp.float32
            )
            probability = mass * gain + (old_mass[at, :] * kept + SMOOTHING / C)
            log_probs = jnp.log(probability)
            logs[at, :] = log_probs
            copies.append(
                pltpu.make_async_copy(logs.at[at], out_ref.at[at], sems.at[i])
            )
            copies[-1].start()
            entropy = entropy - jnp.sum(probability * log_probs, axis=0, keepdims=True)
        stat_ref[...] = entropy
        for copy in copies:
            copy.wait()
    else:
        mass = jnp.dot(onehot[...], weights[...], preferred_element_type=jnp.float32)
        out_ref[...] = mass if first else mass + fade * old_mass[...]
        stat_ref[0:1] = top
        stat_ref[1:2] = total


def attend(pool, labels, state, last):
    depth, count = pool.shape
    first = state is None
    pieces = len(labels)
    m = pieces * 128
    pool = pltpu.with_memory_space_constraint(pool, pltpu.VMEM)
    args = list(labels) + [pool] + ([] if first else list(state))
    scratch = [
        pltpu.VMEM((m, count), jnp.float32),
        pltpu.VMEM((m, count), jnp.bfloat16),
        pltpu.VMEM((C, m), jnp.bfloat16),
    ]
    need = 6 * m * count + 2 * C * m + 4 * C * count
    if first:
        scratch += [
            pltpu.VMEM((pieces,) + labels[0].shape, jnp.bfloat16),
            pltpu.SemaphoreType.DMA((pieces,)),
        ]
    if last:
        scratch += [
            pltpu.VMEM((C, count), jnp.float32),
            pltpu.SemaphoreType.DMA((C // 200,)),
        ]
        need += 4 * C * count
    label_specs = [ANY if first else VMEM] * pieces
    place = jax.ShapeDtypeStruct if last else pltpu.VMEM
    return pl.pallas_call(
        functools.partial(attend_kernel, pieces, first, last, 2.0 * math.log2(math.e) / math.sqrt(depth)),
        in_specs=label_specs + [VMEM] * (len(args) - len(label_specs)),
        out_specs=[ANY if last else VMEM, VMEM],
        out_shape=[
            place((C, count), jnp.float32),
            place((1 if last else 2, count), jnp.float32),
        ],
        scratch_shapes=scratch,
        input_output_aliases={}
        if first or last
        else {pieces + 1: 0, pieces + 2: 1},
        compiler_params=pltpu.CompilerParams(vmem_limit_bytes=52 * 2**20 if first else need + 8 * 2**20),
        cost_estimate=pl.CostEstimate(
            flops=2 * m * count * (depth + C),
            bytes_accessed=4 * C * count,
            transcendentals=m * count,
        ),
    )(*args)


def choose_kernel(up_ref, down_ref, out_ref):
    core = lax.axis_index("c")

    @pl.when(core == 0)
    def _():
        out_ref[...] = down_ref[...]

    @pl.when(core != 0)
    def _():
        out_ref[...] = up_ref[...]


def per_device(pool_embed, label_embed, label_class):
    feats = SIZES[3] * SIZES[4]
    count, width = pool_embed.shape[0] // feats, pool_embed.shape[1]
    rows = label_embed.shape[0]
    own = move(
        pack_kernel,
        (16, rows, width + rows),
        (label_embed, label_class.reshape(1, rows)),
        60,
    )
    parts = lax.all_to_all(own, PLANE, 0, 0, tiled=True)
    own, pool_embed = lax.optimization_barrier((own, pool_embed))
    queries = pool_embed.T.reshape(width, feats, count).transpose(1, 0, 2)
    plane = move(arrange_kernel, (12 * 2 * rows + TAIL, LANES), (parts,))
    plane, queries = lax.optimization_barrier((plane, queries))
    pool = lax.all_to_all(queries, FEAT, 0, 0, tiled=True)
    pool = pool.reshape(feats * width, count)
    got = [plane, swap(plane)]
    up, down = plane, plane
    for _ in range(3):
        up, down = along_z(up, 1), along_z(down, -1)
        got += [up, down, swap(up), swap(down)]
    far = move(choose_kernel, up.shape, (up, down))
    ends = [
        pltpu.with_memory_space_constraint(outward(far, cross), pltpu.VMEM)
        for cross in (0, 1)
    ]
    state = attend(pool, got, None, False)
    log_probs, entropy = attend(pool, ends, state, True)
    return (log_probs.T, entropy[0])


def solution(mesh):
    fine = Mesh(mesh.devices.reshape(SIZES), AXES)
    blk = ("xh", "z", "c")
    return jax.shard_map(
        per_device,
        mesh=fine,
        in_specs=(P(blk, FEAT), P(blk, FEAT), P(blk)),
        out_specs=(P(blk + FEAT, None), P(blk + FEAT)),
        check_vma=False,
    )
```
